512 devices in a mesh: row: 32 (over z_hi, x, y), tp: 16 (over z_lo, core).
Axes of the slice: x: 4, y: 4, z: 16 (z_hi: 2, z_lo: 8; z = z_hi * 8 + z_lo), core: 2. Of those that a mesh axis runs over, the one named last changes fastest.
Arguments:
- tokens: bfloat16 [8192, 4096], P('row', 'tp'), may hold values from -6 to 6
- w_query: bfloat16 [4096, 4096], P(None, 'tp'), may hold values from -0.09375 to 0.09375
- w_keyval: bfloat16 [4096, 4096], P(None, 'tp'), may hold values from -1 to 1, as said below
- prefix_cache: bfloat16 [32, 1024, 4096], P('row', None, 'tp'), may hold values from -1000 to 1000, as said below
- prefix_len: int32 [32], P('row'), may hold values from 2 to 1024, as said below
- page_owner: int32 [512, 2], P('row'), may hold values from 0 to 31, all different within a row; in each aligned block of 16 rows (0 to 15, 16 to 31, ...) at most 2 rows name the same one
Outputs:
- context: bfloat16 [8192, 4096], P('row', 'tp')
- page_store: bfloat16 [2048, 16, 2048], P('row', None, 'tp')
The draws below stay inside these ranges and needn't reach their ends.
Inputs may be any that keep to these rules, and one draw needn't show every extreme that they name: `prefix_len`: no row is given more than 1024 cached positions, and some row exactly 1024. `prefix_cache`: the 2 stored copies of each key head are equal. `w_keyval`: the 2 stored copies of each key head's columns are equal. `page_owner`: the two owners of a page differ. Among the 16 pages of one row no owner is named more than 2 times, and in some row one owner exactly 2 times.
All inputs are finite; a program needn't handle non-finite values.
Results may differ from the reference program's by a relative error of at most 0.025.
Values may be sent and summed in bfloat16 or wider, within the bound.
No kernel may reach another device: no remote copies, remote signals or barrier semaphores. Data moves between devices by JAX's collectives and lax.ppermute only.
A program may use at most 64 MiB of HBM per device.

```python
import math
import jax
import jax.numpy as jnp
import numpy as np
from jax import lax

D = 4096
NH = 32
KVH = 8
HD = 128
PAGE = 16
TOK_DEV = 256
PREFIX = 1024
REP = 2
TOKENS = 8192
PAGES_DEV = 16
MOST = 2
N_ROW = 32


def draw_w_keyval(key, part):
    key = jax.random.fold_in(key, 7)
    base = jax.random.normal(key, (D, KVH, 1, 2 * HD), jnp.float32) * D ** (-0.5)
    base = jnp.clip(base, -1.0, 1.0)
    values = jnp.broadcast_to(base, (D, KVH, REP, 2 * HD))
    return values.reshape(D, KVH * REP * 2 * HD).astype(jnp.bfloat16)


def draw_prefix_cache(key, part):
    key = jax.random.fold_in(key, 11)
    key_base = jax.random.fold_in(key, 0)
    shape = (N_ROW, PREFIX, KVH, 2, HD)
    values = jax.random.normal(key_base, shape, jnp.float32)
    values = jnp.clip(values, -1000.0, 1000.0)
    values = values.reshape(N_ROW, PREFIX, KVH, 1, 2 * HD)
    values = jnp.broadcast_to(values, (N_ROW, PREFIX, KVH, REP, 2 * HD))
    return values.reshape(N_ROW, PREFIX, KVH * REP * 2 * HD).astype(jnp.bfloat16)


def draw_prefix_len(key, part):
    key = jax.random.fold_in(key, 5)
    key_len, key_top = jax.random.split(key, 2)
    lengths = jax.random.randint(key_len, (N_ROW,), 2, PREFIX + 1, jnp.int32)
    longest = jax.random.randint(key_top, (), 0, N_ROW, jnp.int32)
    return jnp.where(jnp.arange(N_ROW, dtype=jnp.int32) == longest, PREFIX, lengths).astype(jnp.int32)


def levels(rng, extent, shards, least, top_value):
    def one(dim, blocks):
        draws = jax.random.uniform(jax.random.fold_in(jax.random.fold_in(rng, 6), dim), (blocks,), jnp.float32, least / len(shards), top_value / len(shards))
        return jnp.repeat(jnp.exp(draws), extent[dim] // blocks).reshape((-1,) + (1,) * (len(extent) - dim - 1))

    loudness = one(*shards[0])
    for cut in shards[1:]:
        loudness = loudness * one(*cut)
    return loudness


def routed_block(rng, own, number, rows, count, top, bound, skew):
    sequence = jax.random.permutation(rng, count)
    crowded, ordinary = portions_of(count, rows * top, bound, skew, True), portions_of(count, rows * top, bound, skew, False)
    places = jnp.arange(count)

    def named(sizes, offset_by):
        used = int((sizes > 0).sum())
        fixed = max(1, used // 4)
        passed = fixed + (places - fixed + offset_by * (used - fixed)) % max(1, count - fixed)
        return jnp.zeros((count,), jnp.int32).at[sequence[jnp.where(places < fixed, places, passed)]].set(jnp.asarray(sizes, jnp.int32))

    sizes = jnp.where(number % 4 == 0, named(crowded, number // 4), named(ordinary, number - number // 4 - 1))
    mixed = jax.random.permutation(jax.random.fold_in(own, 3), count)
    donor, taker = mixed[0:count // 2 * 2:2], mixed[1:count // 2 * 2:2]
    margin = jnp.minimum(sizes[donor] - 1, bound - sizes[taker]) // 2
    margin = jnp.where((donor == sequence[0]) | (taker == sequence[0]) | (sizes[taker] == 0), 0, jnp.maximum(margin, 0))
    passed = jax.random.randint(jax.random.fold_in(own, 4), (count // 2,), 0, 1 << 20) % (margin + 1)
    sizes = sizes.at[donor].add(-passed).at[taker].add(passed)
    labels = jnp.searchsorted(jnp.cumsum(sizes), jnp.arange(rows * top), side="right").astype(jnp.int32)
    table = labels.reshape(top, rows).T
    table = table[jax.random.permutation(jax.random.fold_in(own, 1), rows)]
    offset_by = jax.random.randint(jax.random.fold_in(own, 2), (rows, 1), 0, top)
    return jnp.take_along_axis(table, (jnp.arange(top)[None, :] + offset_by) % top, axis=1)


def portions_of(number_of, total, bound, slope, full):
    portions = [(1 << 20) // math.isqrt(standing ** slope) + 1 for standing in range(1, number_of + 1)]
    largest = bound if full else min(bound, max(-(-total // number_of), total * portions[0] // sum(portions)))
    least = 1 if total - largest >= number_of - 1 else 0
    given, surplus = [largest] + [least] * (number_of - 1), total - largest - least * (number_of - 1)
    while surplus > 0:
        free = [i for i in range(1, number_of) if given[i] < largest] or [i for i in range(1, number_of) if given[i] < bound]
        whole, budget = sum([portions[i] for i in free]), surplus
        for i in free:
            extra = min(bound - given[i], max(1, budget * portions[i] // whole), surplus)
            given[i] = given[i] + extra
            surplus = surplus - extra
    return np.array(given)


def normal_values(stream_key, shape, scale, reach, pieces=(), kind=jnp.bfloat16):
    entries = scale * jax.random.normal(stream_key, shape, jnp.float32)
    if pieces:
        entries = entries * levels(stream_key, shape, pieces, -0.22, 0.18)
    return jnp.clip(entries, -reach, reach).astype(kind)


def setup_inputs(seed: int = 0) -> dict:
    splits = jax.random.split(jax.random.key(seed), 7)
    tokens = normal_values(splits[0], (TOKENS, D), 1.0, 6.0, ((0, 32), (1, 16)))
    w_query = normal_values(splits[1], (D, NH * HD), D ** -0.5, 0.09375, ((1, 16),))
    w_keyval = draw_w_keyval(jax.random.fold_in(splits[6], 71), 0)
    prefix_cache = draw_prefix_cache(jax.random.fold_in(splits[6], 71), 0)
    prefix_len = draw_prefix_len(jax.random.fold_in(splits[6], 71), 0)
    page_owner_keys = jax.random.split(jax.random.fold_in(splits[5], 1), (N_ROW * PAGES_DEV) // PAGES_DEV)
    page_owner_turns = jax.random.permutation(jax.random.fold_in(splits[5], 3), (N_ROW * PAGES_DEV) // PAGES_DEV)
    page_owner = jax.vmap(lambda own, number: routed_block(jax.random.fold_in(splits[5], 2), own, number, PAGES_DEV, N_ROW, 2, MOST, 2))(page_owner_keys, page_owner_turns).reshape((N_ROW * PAGES_DEV, 2))
    return dict(tokens=tokens, w_query=w_query, w_keyval=w_keyval, prefix_cache=prefix_cache, prefix_len=prefix_len, page_owner=page_owner)


ROPE_BASE = 500000.0


def rotate(values, positions):
    half = values.shape[-1] // 2
    inverse = ROPE_BASE ** (-(jnp.arange(half, dtype=jnp.float32) * 2.0 / values.shape[-1]))
    angles = positions[..., None] * inverse
    cosine = jnp.cos(angles)[..., None, :]
    sine = jnp.sin(angles)[..., None, :]
    first = values[..., :half]
    second = values[..., half:]
    return jnp.concatenate([first * cosine - second * sine, second * cosine + first * sine], axis=-1)


def attend_row(inputs):
    queries, new_keys, new_values, cached, length = inputs
    keys = jnp.concatenate([cached[:, :, 0], new_keys], axis=0).astype(jnp.float32)
    values = jnp.concatenate([cached[:, :, 1], new_values], axis=0).astype(jnp.float32)
    scores = jnp.einsum("tkgd,skd->kgts", queries.astype(jnp.float32), keys)
    column = jnp.arange(PREFIX + TOK_DEV, dtype=jnp.int32)[None, :]
    row_ids = jnp.arange(TOK_DEV, dtype=jnp.int32)[:, None]
    valid = jnp.where(column < PREFIX, column < length, column - PREFIX <= row_ids)
    highest = jnp.max(jnp.where(valid, scores, -jnp.inf), axis=-1, keepdims=True)
    weights = jnp.where(valid, jnp.exp(scores - highest), 0.0)
    total = jnp.sum(weights, axis=-1, keepdims=True)
    rounded = lax.optimization_barrier(weights.astype(jnp.bfloat16))
    mixed = jnp.einsum("kgts,skd->kgtd", rounded.astype(jnp.float32), values) / total
    return jnp.transpose(mixed, (2, 0, 1, 3)).reshape(TOK_DEV, NH * HD).astype(jnp.bfloat16)


def reference(tokens, w_query, w_keyval, prefix_cache, prefix_len, page_owner):
    groups = NH // KVH
    columns = KVH * 2 * HD
    wkv = w_keyval.reshape(D, KVH, REP, 2 * HD)[:, :, 0].reshape(D, columns)
    cache = prefix_cache.reshape(N_ROW, PREFIX, KVH, REP, 2 * HD)[:, :, :, 0]
    query = jnp.dot(tokens, w_query, preferred_element_type=jnp.float32).reshape(N_ROW, TOK_DEV, NH, HD)
    keyval = jnp.dot(tokens, wkv, preferred_element_type=jnp.float32).reshape(N_ROW, TOK_DEV, KVH, 2, HD)
    positions = prefix_len.astype(jnp.float32)[:, None] + jnp.arange(TOK_DEV, dtype=jnp.float32)[None, :]
    queries = (rotate(query, positions) * HD ** -0.5).astype(jnp.bfloat16)
    queries = lax.optimization_barrier(queries)
    rotated = rotate(keyval[:, :, :, 0], positions)
    fresh = jnp.stack([rotated, keyval[:, :, :, 1]], axis=3).astype(jnp.bfloat16)
    fresh = lax.optimization_barrier(fresh)
    cached = cache.reshape(N_ROW, PREFIX, KVH, 2, HD)
    context = lax.map(attend_row, (queries.reshape(N_ROW, TOK_DEV, KVH, groups, HD), fresh[:, :, :, 0], fresh[:, :, :, 1], cached, prefix_len))
    context = context.reshape(N_ROW * TOK_DEV, NH * HD)
    pages = fresh.reshape(N_ROW, PAGES_DEV, PAGE * columns)
    owners = page_owner.reshape(N_ROW, 2 * PAGES_DEV).astype(jnp.int32)
    onehot = (owners[:, :, None] == jnp.arange(N_ROW, dtype=jnp.int32)[None, None, :]).astype(jnp.int32)
    earlier = (jnp.cumsum(onehot, axis=1) - onehot).astype(jnp.int32)
    rank = jnp.sum(earlier * onehot, axis=2).astype(jnp.int32)
    source = jnp.arange(N_ROW, dtype=jnp.int32)[:, None]
    target = (owners * (N_ROW * MOST) + source * MOST + rank).astype(jnp.int32)
    copies = jnp.repeat(pages, 2, axis=1).reshape(N_ROW * 2 * PAGES_DEV, PAGE * columns)
    store = jnp.zeros((N_ROW * N_ROW * MOST, PAGE * columns), jnp.bfloat16).at[target.reshape(-1)].set(copies)
    return context, store.reshape(N_ROW * N_ROW * MOST, PAGE, columns)
```

```python
import functools
import jax
import jax.numpy as jnp
from jax import lax
from jax.experimental import pallas as pl
from jax.experimental.pallas import tpu as pltpu
from jax.sharding import PartitionSpec as P

HD = 128
PAGE = 16
ROPE_BASE = 500000.0
CHIPS = 8
ROWS = 256
BLOCK = 512
STEPS = ((3, 0), (1, 0), (2, 1), (4, 3), (6, 3), (5, 4), (7, 6))
EARLY = (1, 2, 3, 4)
LATE = (5, 6, 7)
BF = jnp.bfloat16
F32 = jnp.float32


def step_perm(got, held):
    hop = got - held
    right = [(2 * c, 2 * (c + hop)) for c in range(CHIPS) if c >= held and c + hop < CHIPS]
    left = [
        (2 * c + 1, 2 * (c - hop) + 1) for c in range(CHIPS) if c + held < CHIPS and c >= hop
    ]
    return right + left


def partial_kernel(count, first, rows_ref, *refs):
    blocks, refs = refs[:count], refs[count:]
    weights, refs = refs[:3], refs[3:]
    given, outs = refs[: len(refs) - 3], refs[len(refs) - 3 :]
    step = pl.program_id(0)

    def add(block):
        for j in range(3):
            product = jnp.dot(block[0:ROWS], weights[j][0:256], preferred_element_type=F32)
            product += jnp.dot(block[ROWS:], weights[j][256:], preferred_element_type=F32)
            outs[j][...] += product

    @pl.when(step == 0)
    def _():
        if first:
            own, given_weights = given[0], given[1:]
            for j in range(3):
                outs[j][...] = jnp.dot(
                    own[...], given_weights[j][...], preferred_element_type=F32
                )
        else:
            for j in range(3):
                outs[j][...] = given[j][...]

    for s in range(count):
        pl.when(step == s)(functools.partial(add, blocks[s]))


def partial_sums(rows, blocks, weights, given, first):
    count = len(blocks)
    whole = lambda s, r: (0, 0)
    in_specs = [pl.BlockSpec((2 * ROWS, 256), whole)] * count
    in_specs += [pl.BlockSpec((BLOCK, 256), lambda s, r: (r[s], 0))] * 3
    if first:
        in_specs += [pl.BlockSpec((ROWS, 256), whole)]
        in_specs += [pl.BlockSpec((256, 256), lambda s, r: (r[count], 0))] * 3
        given = [given] + list(weights)
    else:
        in_specs += [pl.BlockSpec((ROWS, 256), whole)] * 3
    return pl.pallas_call(
        functools.partial(partial_kernel, count, first),
        out_shape=[jax.ShapeDtypeStruct((ROWS, 256), F32)] * 3,
        grid_spec=pltpu.PrefetchScalarGridSpec(
            num_scalar_prefetch=1,
            grid=(count,),
            in_specs=in_specs,
            out_specs=[pl.BlockSpec((ROWS, 256), whole)] * 3,
        ),
        compiler_params=pltpu.CompilerParams(vmem_limit_bytes=24 << 20),
        cost_estimate=pl.CostEstimate(
            flops=2 * ROWS * BLOCK * 768 * count,
            bytes_accessed=count * 1024 * 1024 + 3 * 262144,
            transcendentals=0,
        ),
        name="partial_sums",
    )(rows, *blocks, *weights, *given)


def rotate_kernel(core_ref, q_ref, kv_ref, got_ref, cos_ref, sin_ref, tag_ref, query_ref, fresh_ref, page_ref):
    cosine, sine = cos_ref[...], sin_ref[...]

    def rotated(v):
        return v * cosine + pltpu.roll(v, HD // 2, 1) * sine

    for h in range(2):
        at = slice(h * HD, (h + 1) * HD)
        query = q_ref[:, at] + got_ref[:, at]
        query_ref[h * ROWS : (h + 1) * ROWS, :] = (rotated(query) * HD**-0.5).astype(BF)
    key = rotated(kv_ref[:, :HD] + got_ref[:, 256 : 256 + HD]).astype(BF)
    value = (kv_ref[:, HD:] + got_ref[:, 256 + HD :]).astype(BF)
    fresh_ref[:, :HD] = key
    fresh_ref[:, HD:] = value
    page_ref[0:ROWS, :] = jnp.where(core_ref[0] == 0, key.astype(F32), value.astype(F32)).astype(BF)
    page_ref[ROWS:, :] = tag_ref[...]


def attend_kernel(len_ref, query_ref, fresh_ref, cache_ref, out_ref):
    queries = query_ref[...]
    contract = (((1,), (1,)), ((), ()))
    old = lax.dot_general(queries, cache_ref[:, :HD], contract, preferred_element_type=F32)
    new = lax.dot_general(queries, fresh_ref[:, :HD], contract, preferred_element_type=F32)
    column = lax.broadcasted_iota(jnp.int32, old.shape, 1)
    old = jnp.where(column < len_ref[0], old, -jnp.inf)
    token = lax.broadcasted_iota(jnp.int32, new.shape, 0) & (ROWS - 1)
    column = lax.broadcasted_iota(jnp.int32, new.shape, 1)
    new = jnp.where(column <= token, new, -jnp.inf)
    highest = jnp.maximum(
        jnp.max(old, axis=1, keepdims=True), jnp.max(new, axis=1, keepdims=True)
    )
    old = jnp.exp(old - highest)
    new = jnp.exp(new - highest)
    total = jnp.sum(old, axis=1, keepdims=True) + jnp.sum(new, axis=1, keepdims=True)
    mixed = jnp.dot(old.astype(BF), cache_ref[:, HD:], preferred_element_type=F32)
    mixed += jnp.dot(new.astype(BF), fresh_ref[:, HD:], preferred_element_type=F32)
    result = (mixed / total).astype(BF)
    out_ref[:, :HD] = result[:ROWS]
    out_ref[:, HD:] = result[ROWS:]


def pack_kernel(own_ref, tag_ref, got_ref, out_ref):
    lane = lax.broadcasted_iota(jnp.int32, (1, ROWS), 1)
    within = lax.rem(lane, PAGE)
    rows = out_ref.shape[0]
    row = lax.broadcasted_iota(jnp.int32, (rows, ROWS), 0)

    def placed(tags):
        slots = tags.astype(F32).astype(jnp.int32)
        hit = None
        for copy in range(2):
            slot = jnp.concatenate([slots[2 * copy : 2 * copy + 1], slots[2 * copy + 1 : 2 * copy + 2]], axis=1)
            same = row == slot * PAGE + within
            hit = same if hit is None else hit | same
        return jnp.where(hit, 1.0, 0.0).astype(BF)

    out = jnp.dot(placed(tag_ref[...]), own_ref[0:ROWS, :], preferred_element_type=F32)
    out += jnp.dot(placed(got_ref[ROWS:, :]), got_ref[0:ROWS, :], preferred_element_type=F32)
    out_ref[...] = out.astype(BF)


def shards(tokens, w_query, w_keyval, prefix_cache, prefix_len, page_owner):
    place = lax.axis_index("tp")
    row = lax.axis_index("row")
    chip, core = place // 2, place % 2
    half, pages = row // 16, page_owner.shape[0]
    siblings = [(t, t ^ 1) for t in range(2 * CHIPS)]

    mine = lax.all_gather(
        tokens, "tp", axis=0, tiled=True,
        axis_index_groups=[[2 * c, 2 * c + 1] for c in range(CHIPS)],
    )
    held = {0: mine}
    for got, had in STEPS:
        held[got] = lax.ppermute(held[had], "tp", step_perm(got, had))
    w_other = lax.ppermute(w_query, "tp", siblings)

    inverse = ROPE_BASE ** (-(jnp.arange(HD // 2, dtype=F32) * 2.0 / HD))
    positions = prefix_len[0].astype(F32) + jnp.arange(ROWS, dtype=F32)
    angles = positions[:, None] * inverse
    cosine, sine = jnp.cos(angles), jnp.sin(angles)
    cosine = jnp.concatenate([cosine, cosine], axis=1)
    sine = jnp.concatenate([-sine, sine], axis=1)
    owner = page_owner.reshape(-1)
    same = owner[:, None] == owner[None, :]
    earlier = jnp.arange(2 * pages)[None, :] < jnp.arange(2 * pages)[:, None]
    rank = jnp.sum((same & earlier).astype(jnp.int32), axis=1)
    slot = (owner % 16) * 4 + half * 2 + rank

    def tags(target):
        kept = jnp.where(owner // 16 == target, slot, 128).reshape(pages, 2)
        lanes = jnp.repeat(kept.T, PAGE, axis=1).reshape(4, HD)
        return jnp.concatenate([lanes, jnp.full((12, HD), 128, jnp.int32)], axis=0).astype(BF)

    own_tags, sent_tags = tags(half), tags(1 - half)

    def block_of(offset):
        return jnp.clip(jnp.where(core == 0, chip - offset, chip + offset), 0, CHIPS - 1)

    early = jnp.stack([block_of(k) for k in EARLY] + [place]).astype(jnp.int32)
    late = jnp.stack([block_of(k) for k in LATE]).astype(jnp.int32)
    weights = [w_query, w_other, w_keyval]
    sums = partial_sums(early, [held[k] for k in EARLY], weights, tokens, True)
    query, other, keyval = partial_sums(late, [held[k] for k in LATE], weights, sums, False)
    got = lax.ppermute(jnp.concatenate([other, keyval], axis=1), "tp", siblings)

    queries, fresh, page = pl.pallas_call(
        rotate_kernel,
        out_shape=[
            jax.ShapeDtypeStruct((2 * ROWS, HD), BF),
            jax.ShapeDtypeStruct((ROWS, 2 * HD), BF),
            jax.ShapeDtypeStruct((ROWS + 16, HD), BF),
        ],
        in_specs=[pl.BlockSpec(memory_space=pltpu.SMEM)] + [pl.BlockSpec()] * 6,
        name="rotate",
    )(core.reshape(1).astype(jnp.int32), query, keyval, got, cosine, sine, sent_tags)

    far = lax.ppermute(page, "row", [(r, (r + 16) % 32) for r in range(32)])
    context = pl.pallas_call(
        attend_kernel,
        out_shape=jax.ShapeDtypeStruct((ROWS, 2 * HD), BF),
        in_specs=[pl.BlockSpec(memory_space=pltpu.SMEM)] + [pl.BlockSpec()] * 3,
        compiler_params=pltpu.CompilerParams(vmem_limit_bytes=40 << 20),
        cost_estimate=pl.CostEstimate(flops=400_000_000, bytes_accessed=1_000_000, transcendentals=700_000),
        name="attend",
    )(prefix_len, queries, fresh, prefix_cache[0])
    packed = pl.pallas_call(
        pack_kernel,
        out_shape=jax.ShapeDtypeStruct((64 * PAGE, HD), BF),
        compiler_params=pltpu.CompilerParams(vmem_limit_bytes=24 << 20),
        name="pack",
    )(page, own_tags, far)
    received = lax.all_to_all(
        packed, "row", 0, 0, tiled=True,
        axis_index_groups=[[z * 16 + i for i in range(16)] for z in range(2)],
    )
    store = received.reshape(16, 2, 2, PAGE, HD).transpose(1, 0, 2, 3, 4)
    return context, store.reshape(64, PAGE, HD)


def solution(mesh):
    return jax.shard_map(
        shards,
        mesh=mesh,
        in_specs=(
            P("row", "tp"),
            P(None, "tp"),
            P(None, "tp"),
            P("row", None, "tp"),
            P("row"),
            P("row", None),
        ),
        out_specs=(P("row", "tp"), P("row", None, "tp")),
        check_vma=False,
    )
```

```python
import functools
import jax
import jax.numpy as jnp
from jax import lax
from jax.experimental import pallas as pl
from jax.experimental.pallas import tpu as pltpu
from jax.sharding import PartitionSpec as P

HD = 128
PAGE = 16
ROPE_BASE = 500000.0
CHIPS = 8
ROWS = 256
BLOCK = 512
VMEM = pl.BlockSpec(memory_space=pltpu.VMEM)
SMEM = pl.BlockSpec(memory_space=pltpu.SMEM)
BF = jnp.bfloat16
F32 = jnp.float32


def step_perm(got, held):
    hop = got - held
    right = [(2 * c, 2 * (c + hop)) for c in range(CHIPS) if c >= held and c + hop < CHIPS]
    left = [
        (2 * c + 1, 2 * (c - hop) + 1) for c in range(CHIPS) if c + held < CHIPS and c >= hop
    ]
    return right + left


def partial_kernel(offsets, own, rows_ref, *refs):
    count = len(offsets)
    blocks, weights, refs = refs[:count], refs[count : count + 3], refs[count + 3 :]
    given, (keep_ref, send_ref) = refs[:-2], refs[-2:]

    def terms(block, start, depth):
        at = pl.ds(pl.multiple_of(start, depth), depth)
        return [jnp.dot(block, w[at, :], preferred_element_type=F32) for w in weights]

    if own:
        sums = terms(given[0][...], rows_ref[0] * ROWS, ROWS)
    else:
        sums = [given[0][...], given[1][:, :256], given[1][:, 256:]]
    for block, offset in zip(blocks, offsets):
        both = jnp.concatenate([block[:ROWS], block[ROWS:]], axis=1)
        found = terms(both, rows_ref[offset] * BLOCK, BLOCK)
        sums = [x + y for x, y in zip(sums, found)]
    keep_ref[...] = sums[0]
    send_ref[:, :256] = sums[1]
    send_ref[:, 256:] = sums[2]


def partial_sums(rows, offsets, blocks, weights, given, own):
    operands = [*blocks, *weights, *given]
    return pl.pallas_call(
        functools.partial(partial_kernel, offsets, own),
        out_shape=[
            jax.ShapeDtypeStruct((ROWS, 256), F32),
            jax.ShapeDtypeStruct((ROWS, 512), F32),
        ],
        in_specs=[SMEM] + [VMEM] * len(operands),
        out_specs=[VMEM] * 2,
        compiler_params=pltpu.CompilerParams(vmem_limit_bytes=16 << 20),
        cost_estimate=pl.CostEstimate(
            flops=2 * ROWS * BLOCK * 768 * len(offsets),
            bytes_accessed=len(offsets) * 1024 * 1024,
            transcendentals=0,
        ),
        name="partial_sums",
    )(rows, *operands)


def rotate_kernel(
    core_ref, q_ref, sent_ref, got_ref, cos_ref, sin_ref, tag_ref, query_ref, fresh_ref, page_ref
):
    cosine, sine = cos_ref[...], sin_ref[...]

    def rotated(v):
        return v * cosine + pltpu.roll(v, HD // 2, 1) * sine

    for h in range(2):
        at = slice(h * HD, (h + 1) * HD)
        query = q_ref[:, at] + got_ref[:, at]
        query_ref[h * ROWS : (h + 1) * ROWS, :] = (rotated(query) * HD**-0.5).astype(BF)
    key = rotated(sent_ref[:, 256 : 256 + HD] + got_ref[:, 256 : 256 + HD]).astype(BF)
    value = (sent_ref[:, 256 + HD :] + got_ref[:, 256 + HD :]).astype(BF)
    fresh_ref[:, :HD] = key
    fresh_ref[:, HD:] = value
    page_ref[0:ROWS, :] = jnp.where(core_ref[0] == 0, key.astype(F32), value.astype(F32)).astype(BF)
    page_ref[ROWS:, :] = tag_ref[...]


def attend_kernel(len_ref, query_ref, fresh_ref, cache_ref, out_ref):
    queries = query_ref[...]
    contract = (((1,), (1,)), ((), ()))
    old = lax.dot_general(queries, cache_ref[:, :HD], contract, preferred_element_type=F32)
    new = lax.dot_general(queries, fresh_ref[:, :HD], contract, preferred_element_type=F32)
    column = lax.broadcasted_iota(jnp.int32, old.shape, 1)
    old = jnp.where(column < len_ref[0], old, -jnp.inf)
    token = lax.broadcasted_iota(jnp.int32, new.shape, 0) & (ROWS - 1)
    column = lax.broadcasted_iota(jnp.int32, new.shape, 1)
    new = jnp.where(column <= token, new, -jnp.inf)
    highest = jnp.maximum(
        jnp.max(old, axis=1, keepdims=True), jnp.max(new, axis=1, keepdims=True)
    )
    old = jnp.exp(old - highest)
    new = jnp.exp(new - highest)
    total = jnp.sum(old, axis=1, keepdims=True) + jnp.sum(new, axis=1, keepdims=True)
    mixed = jnp.dot(old.astype(BF), cache_ref[:, HD:], preferred_element_type=F32)
    mixed += jnp.dot(new.astype(BF), fresh_ref[:, HD:], preferred_element_type=F32)
    result = (mixed / total).astype(BF)
    out_ref[:, :HD] = result[:ROWS]
    out_ref[:, HD:] = result[ROWS:]


def pack_kernel(own_ref, tag_ref, got_ref, out_ref):
    lane = lax.broadcasted_iota(jnp.int32, (1, ROWS), 1)
    within = lax.rem(lane, PAGE)
    rows = out_ref.shape[0]
    row = lax.broadcasted_iota(jnp.int32, (rows, ROWS), 0)

    def placed(tags):
        slots = tags.astype(F32).astype(jnp.int32)
        hit = None
        for copy in range(2):
            slot = jnp.concatenate([slots[2 * copy : 2 * copy + 1], slots[2 * copy + 1 : 2 * copy + 2]], axis=1)
            same = row == slot * PAGE + within
            hit = same if hit is None else hit | same
        return jnp.where(hit, 1.0, 0.0).astype(BF)

    out = jnp.dot(placed(tag_ref[...]), own_ref[0:ROWS, :], preferred_element_type=F32)
    out += jnp.dot(placed(got_ref[ROWS:, :]), got_ref[0:ROWS, :], preferred_element_type=F32)
    out_ref[...] = out.astype(BF)


def shards(tokens, w_query, w_keyval, prefix_cache, prefix_len, page_owner):
    place = lax.axis_index("tp")
    row = lax.axis_index("row")
    chip, core = place // 2, place % 2
    half, pages = row // 16, page_owner.shape[0]
    siblings = [(t, t ^ 1) for t in range(2 * CHIPS)]

    mine = lax.all_gather(
        tokens, "tp", axis=0, tiled=True,
        axis_index_groups=[[2 * c, 2 * c + 1] for c in range(CHIPS)],
    )
    inverse = ROPE_BASE ** (-(jnp.arange(HD // 2, dtype=F32) * 2.0 / HD))
    positions = prefix_len[0].astype(F32) + jnp.arange(ROWS, dtype=F32)
    angles = positions[:, None] * inverse
    cosine, sine = jnp.cos(angles), jnp.sin(angles)
    cosine = jnp.concatenate([cosine, cosine], axis=1)
    sine = jnp.concatenate([-sine, sine], axis=1)
    owner = page_owner.reshape(-1)
    same = owner[:, None] == owner[None, :]
    earlier = jnp.arange(2 * pages)[None, :] < jnp.arange(2 * pages)[:, None]
    rank = jnp.sum((same & earlier).astype(jnp.int32), axis=1)
    slot = (owner % 16) * 4 + half * 2 + rank

    def tags(target):
        kept = jnp.where(owner // 16 == target, slot, 128).reshape(pages, 2)
        lanes = jnp.repeat(kept.T, PAGE, axis=1).reshape(4, HD)
        return jnp.concatenate([lanes, jnp.full((12, HD), 128, jnp.int32)], axis=0).astype(BF)

    own_tags, sent_tags = tags(half), tags(1 - half)

    def block_of(offset):
        return jnp.clip(jnp.where(core == 0, chip - offset, chip + offset), 0, CHIPS - 1)

    rows = jnp.stack([place] + [block_of(k) for k in range(1, CHIPS)]).astype(jnp.int32)
    held = {0: mine}

    def receive(got, had):
        held[got] = lax.ppermute(held[had], "tp", step_perm(got, had))

    w_sent, _ = lax.optimization_barrier((w_query, mine))
    w_other = lax.ppermute(w_sent, "tp", siblings)
    weights = [
        pltpu.with_memory_space_constraint(w, pltpu.VMEM) for w in (w_query, w_other, w_keyval)
    ]
    receive(3, 0)
    receive(1, 0)
    rows, cosine, sine, own_tags, sent_tags = lax.optimization_barrier(
        (rows, cosine, sine, own_tags, sent_tags)
    )
    sums = partial_sums(rows, (), [], weights, [tokens], True)
    sums, cosine, sine, own_tags, sent_tags, held[3] = lax.optimization_barrier(
        (sums, cosine, sine, own_tags, sent_tags, held[3])
    )
    receive(2, 1)
    receive(4, 3)
    receive(6, 3)
    receive(5, 4)

    def add(offsets, given):
        blocks = [held[k] for k in offsets]
        return partial_sums(rows, offsets, blocks, weights, given, False)

    sums = add((1, 3), sums)
    sums, held[6] = lax.optimization_barrier((sums, held[6]))
    receive(7, 6)
    sums = add((2, 4, 6), sums)
    query, sent = add((7, 5), sums)
    got = lax.ppermute(sent, "tp", siblings)

    queries, fresh, page = pl.pallas_call(
        rotate_kernel,
        out_shape=[
            jax.ShapeDtypeStruct((2 * ROWS, HD), BF),
            jax.ShapeDtypeStruct((ROWS, 2 * HD), BF),
            jax.ShapeDtypeStruct((ROWS + 16, HD), BF),
        ],
        in_specs=[SMEM] + [VMEM] * 6,
        out_specs=[VMEM] * 3,
        compiler_params=pltpu.CompilerParams(vmem_limit_bytes=16 << 20),
        name="rotate",
    )(core.reshape(1).astype(jnp.int32), query, sent, got, cosine, sine, sent_tags)

    far = lax.ppermute(page, "row", [(r, (r + 16) % 32) for r in range(32)])
    context = pl.pallas_call(
        attend_kernel,
        out_shape=jax.ShapeDtypeStruct((ROWS, 2 * HD), BF),
        in_specs=[SMEM] + [VMEM] * 3,
        out_specs=VMEM,
        compiler_params=pltpu.CompilerParams(vmem_limit_bytes=32 << 20),
        cost_estimate=pl.CostEstimate(flops=400_000_000, bytes_accessed=1_000_000, transcendentals=700_000),
        name="attend",
    )(prefix_len, queries, fresh, prefix_cache[0])
    packed = pl.pallas_call(
        pack_kernel,
        out_shape=jax.ShapeDtypeStruct((64 * PAGE, HD), BF),
        in_specs=[VMEM] * 3,
        out_specs=VMEM,
        compiler_params=pltpu.CompilerParams(vmem_limit_bytes=16 << 20),
        name="pack",
    )(page, own_tags, far)
    received = lax.all_to_all(
        packed, "row", 0, 0, tiled=True,
        axis_index_groups=[[z * 16 + i for i in range(16)] for z in range(2)],
    )
    store = received.reshape(16, 2, 2, PAGE, HD).transpose(1, 0, 2, 3, 4)
    return context, store.reshape(64, PAGE, HD)


def solution(mesh):
    return jax.shard_map(
        shards,
        mesh=mesh,
        in_specs=(
            P("row", "tp"),
            P(None, "tp"),
            P(None, "tp"),
            P("row", None, "tp"),
            P("row"),
            P("row", None),
        ),
        out_specs=(P("row", "tp"), P("row", None, "tp")),
        check_vma=False,
    )
```
